768 devices in a mesh: obs: 96 (over y, z), grid: 8 (over x, core).
Axes of the slice: x: 4, y: 8, z: 12, core: 2. Of those that a mesh axis runs over, the one named last changes fastest.
Arguments:
- queries: bfloat16 [196608, 1024], P(('obs', 'grid')), may hold values from -48 to 48
- latent_kv: bfloat16 [8, 384, 2048], P('grid'), may hold values from -4 to 4
- pair_blocks: int32 [1536, 4], P(('obs', 'grid')), may hold values from 0 to 23, as said below
- pair_count: int32 [1536], P(('obs', 'grid')), may hold values from 1 to 4
- obs_count: int32 [1536], P(('obs', 'grid')), may hold values from 32 to 128
- cotangent: bfloat16 [196608, 1024], P(('obs', 'grid')), may hold values from -6 to 6
Outputs:
- attended: bfloat16 [196608, 1024], P(('obs', 'grid'))
- grad_query: bfloat16 [196608, 1024], P(('obs', 'grid'))
- grad_kv: float32 [8, 384, 2048], P('grid', 'obs')
The draws below stay inside these ranges and needn't reach their ends.
Inputs may be any that keep to these rules, and one draw needn't show every extreme that they name: `pair_blocks`: obs block n lies in region (n // 2) % 8. Each entry names a patch block b of that region (b // 3 equal to it), or the last patch block of the region before it, or the first patch block of the region after it, regions counted cyclically. Entries of one obs block may repeat.
All inputs are finite; a program needn't handle non-finite values.
Results may differ from the reference program's by a relative error of at most 0.012.
Values may be sent and summed in bfloat16 or wider, within the bound.
A program may use at most 64 MiB of HBM per device.

```python
import math
import jax
import jax.numpy as jnp
from jax import lax

D = 1024
H = 16
BLOCK = 128
PAIRS = 4
BLK_DEV = 2
LAT_BLK = 3
LAT_REG = 384
REGIONS = 8
NBLK = 1536
NOBS = 196608


def draw_latent_kv(key, part):
    key = jax.random.fold_in(key, 7)
    values = jax.random.normal(key, (REGIONS, LAT_REG, 2 * D), jnp.float32)
    return jnp.clip(values, -4.0, 4.0).astype(jnp.bfloat16)


def draw_queries(key, part):
    key = jax.random.fold_in(key, 9)
    values = jax.random.normal(key, (NOBS, D), jnp.float32)
    return jnp.clip(values, -4.0, 4.0).astype(jnp.bfloat16)


def draw_pair_blocks(key, part):
    key = jax.random.fold_in(key, 11)
    region = (jnp.arange(NBLK, dtype=jnp.int32) // BLK_DEV % REGIONS)[:, None]
    slot_pick = jax.random.randint(key, (NBLK, PAIRS), 0, LAT_BLK + 2)
    before = (region - 1) % REGIONS * LAT_BLK + LAT_BLK - 1
    after = (region + 1) % REGIONS * LAT_BLK
    inside = region * LAT_BLK + slot_pick - 1
    return jnp.where(slot_pick == 0, before, jnp.where(slot_pick == LAT_BLK + 1, after, inside)).astype(jnp.int32)


def set_ends(entries, key, least, high):
    place = [jax.random.randint(jax.random.fold_in(key, axis), (), 0, length) for axis, length in enumerate(entries.shape)]
    widest = entries.shape.index(max(entries.shape))
    beside = place[:widest] + [(place[widest] + 1) % entries.shape[widest]] + place[widest + 1:]
    return entries.at[tuple(place)].set(least).at[tuple(beside)].set(high)


def steps_of(rng, extent, cuts, low, largest):
    gain = 1.0
    for axis_at, blocks in cuts:
        steps = jax.random.uniform(jax.random.fold_in(jax.random.fold_in(rng, 6), axis_at), (blocks,), jnp.float32, low / len(cuts), largest / len(cuts))
        gain = gain * jnp.repeat(jnp.exp(steps), extent[axis_at] // blocks).reshape((-1,) + (1,) * (len(extent) - 1 - axis_at))
    return gain


def bell_draw(stream_key, extent, width, limit, pieces=(), kind=jnp.bfloat16):
    result = width * jax.random.normal(stream_key, extent, jnp.float32)
    if pieces:
        result = result * steps_of(stream_key, extent, pieces, -0.22, 0.18)
    return jnp.clip(result, -limit, limit).astype(kind)


def setup_inputs(seed: int = 0) -> dict:
    arg_keys = jax.random.split(jax.random.key(seed), 7)
    queries = draw_queries(jax.random.fold_in(arg_keys[6], 71), 0)
    latent_kv = draw_latent_kv(jax.random.fold_in(arg_keys[6], 71), 0)
    pair_blocks = draw_pair_blocks(jax.random.fold_in(arg_keys[6], 71), 0)
    pair_count = set_ends(jax.random.randint(arg_keys[3], (NBLK,), 1, PAIRS + 1), jax.random.fold_in(arg_keys[3], 1), 1, PAIRS).astype(jnp.int32)
    obs_count = set_ends(jax.random.randint(arg_keys[4], (NBLK,), BLOCK // 4, BLOCK + 1), jax.random.fold_in(arg_keys[4], 1), BLOCK // 4, BLOCK).astype(jnp.int32)
    cotangent = bell_draw(arg_keys[5], (NOBS, D), 1.0, 6.0, ((0, 768),))
    return {"queries": queries, "latent_kv": latent_kv, "pair_blocks": pair_blocks, "pair_count": pair_count, "obs_count": obs_count, "cotangent": cotangent}


def block_pass(query_rows, kv_rows, key_valid, row_valid, grad_rows):
    feature_count = query_rows.shape[-1]
    head_dim = feature_count // H
    score_scale = 1.0 / math.sqrt(head_dim)
    query_heads = query_rows.astype(jnp.float32).reshape(query_rows.shape[0], H, head_dim)
    key_heads = kv_rows[:, :feature_count].astype(jnp.float32).reshape(kv_rows.shape[0], H, head_dim)
    value_heads = kv_rows[:, feature_count:].astype(jnp.float32).reshape(kv_rows.shape[0], H, head_dim)
    scores = jnp.einsum('qhd,khd->hqk', query_heads, key_heads) * score_scale
    scores = jnp.where(key_valid[None, None, :], scores, -1e+30)
    row_max = lax.optimization_barrier(jnp.max(scores, axis=-1, keepdims=True))
    expanded = jnp.exp(scores - row_max)
    attention = expanded / lax.optimization_barrier(jnp.sum(expanded, axis=-1, keepdims=True))
    attention_low = lax.optimization_barrier(attention.astype(jnp.bfloat16)).astype(jnp.float32)
    mixed = jnp.einsum('hqk,khd->qhd', attention_low, value_heads).reshape(query_rows.shape[0], feature_count)
    attended = jnp.where(row_valid[:, None], mixed, 0.0).astype(jnp.bfloat16)
    grad_heads = jnp.where(row_valid[:, None], grad_rows, 0).astype(jnp.float32).reshape(query_heads.shape)
    grad_values = jnp.einsum('hqk,qhd->khd', attention_low, grad_heads)
    grad_attention = jnp.einsum('qhd,khd->hqk', grad_heads, value_heads)
    delta_term = lax.optimization_barrier(jnp.sum(attention * grad_attention, axis=-1, keepdims=True))
    grad_scores = attention * (grad_attention - delta_term) * score_scale
    grad_low = lax.optimization_barrier(grad_scores.astype(jnp.bfloat16)).astype(jnp.float32)
    grad_query = jnp.einsum('hqk,khd->qhd', grad_low, key_heads).reshape(query_rows.shape[0], feature_count)
    grad_keys = jnp.einsum('hqk,qhd->khd', grad_low, query_heads)
    grad_kv = jnp.concatenate([grad_keys.reshape(kv_rows.shape[0], feature_count), grad_values.reshape(kv_rows.shape[0], feature_count)], axis=1)
    return (attended, grad_query.astype(jnp.bfloat16), grad_kv)

def reference(queries, latent_kv, pair_blocks, pair_count, obs_count, cotangent):
    kv_blocks = latent_kv.reshape(REGIONS * LAT_BLK, BLOCK, 2 * D)
    group_count = NBLK // BLK_DEV
    query_groups = queries.reshape(group_count, BLK_DEV, BLOCK, D)
    grad_groups = cotangent.reshape(group_count, BLK_DEV, BLOCK, D)
    pair_groups = pair_blocks.reshape(group_count, BLK_DEV, PAIRS)
    count_groups = pair_count.reshape(group_count, BLK_DEV)
    valid_groups = obs_count.reshape(group_count, BLK_DEV)
    slot_rows = jnp.arange(PAIRS * BLOCK, dtype=jnp.int32) // BLOCK
    row_index = jnp.arange(BLOCK, dtype=jnp.int32)

    def one_block(query_rows, pair_ids, live_pairs, live_rows, grad_rows):
        kv_rows = kv_blocks[pair_ids].reshape(PAIRS * BLOCK, 2 * D)
        return block_pass(query_rows, kv_rows, slot_rows < live_pairs, row_index < live_rows, grad_rows)

    def advance(accumulated, inputs):
        query_rows, pair_ids, live_pairs, live_rows, grad_rows = inputs
        attended, grad_query, grad_kv = jax.vmap(one_block)(query_rows, pair_ids, live_pairs, live_rows, grad_rows)
        accumulated = accumulated.at[pair_ids.reshape(-1)].add(grad_kv.reshape(BLK_DEV * PAIRS, BLOCK, 2 * D))
        return (accumulated, (attended, grad_query))
    initial = jnp.zeros((REGIONS * LAT_BLK, BLOCK, 2 * D), jnp.float32)
    accumulated, (attended, grad_query) = lax.scan(advance, initial, (query_groups, pair_groups, count_groups, valid_groups, grad_groups))
    return (attended.reshape(NOBS, D), grad_query.reshape(NOBS, D), accumulated.reshape(REGIONS, LAT_REG, 2 * D))
```

```python
import functools
import math

import jax
import jax.numpy as jnp
from jax import lax
from jax.experimental import pallas as pl
from jax.experimental.pallas import tpu as pltpu
from jax.sharding import PartitionSpec as P

H = 16
HEAD = 64
NY, NZ = 8, 12
BLOCK = 128
WIN = 5
QUADS = 4
HEADS = H // QUADS
QUAD = HEADS * HEAD
MESH = pl.DeviceIdType.MESH
SCALE = 1.0 / math.sqrt(HEAD)
LOG2E = 1.4426950408889634
F32, BF16 = jnp.float32, jnp.bfloat16
FIRST_AXIS = ("y", "z", "y", "y")


def dot(a, b):
    return jnp.dot(a, b, preferred_element_type=F32)


def slot_bias(blocks_ref, count_ref, region, n, w, total):
    wanted = lax.rem(3 * region - 1 + w + total, total)
    uses = 0
    for p in range(blocks_ref.shape[1]):
        live = (blocks_ref[n, p] == wanted) & (p < count_ref[n])
        uses = uses + jnp.where(live, 1, 0)
    return jnp.where(
        uses == 0,
        F32(-1e30),
        jnp.where(
            uses == 1,
            F32(0.0),
            jnp.where(uses == 2, F32(1.0), jnp.where(uses == 3, F32(math.log2(3.0)), F32(2.0))),
        ),
    )


def owner_tiles(keys, values):
    rows = keys.shape[0]
    low = lax.broadcasted_iota(jnp.int32, (rows // 8, 8, 128), 1) < 4

    def split(a, lane):
        return a[:, lane : lane + 128].reshape(rows // 8, 8, 128)

    def pair(a):
        left, right = split(a, 0), split(a, 128)
        even = jnp.where(low, left, pltpu.roll(right, 4, 1))
        odd = jnp.where(low, pltpu.roll(left, 4, 1), right)
        return even, odd

    key_even, key_odd = pair(keys)
    value_even, value_odd = pair(values)
    even = jnp.concatenate([key_even, value_even], axis=1)
    odd = jnp.concatenate([key_odd, value_odd], axis=1)
    return jnp.stack([even, odd], axis=1).reshape(rows // 4, 16, 128)


def kernel(
    queries, latent, blocks, pair_count, obs_count, cotangent,
    attended, grad_query, grad_kv,
    window, middle, rim_out, rim_in, part, first_in, second_out, second_in,
    local_sem, halo_send, halo_recv, rim_send, rim_recv,
    first_send, first_recv, second_send, second_recv,
):
    place, region = lax.axis_index("obs"), lax.axis_index("grid")
    regions = lax.axis_size("grid")
    y, z = place // NZ, lax.rem(place, NZ)
    after = (place, lax.rem(region + 1, regions))
    before = (place, lax.rem(region + regions - 1, regions))

    def along(axis, k):
        if axis == "y":
            return lax.rem(y + k, NY)
        return lax.rem(z + k, NZ)

    def peer(axis, k):
        if axis == "y":
            return (along(axis, k) * NZ + z, region)
        return (y * NZ + along(axis, k), region)

    peers = [peer("y", k) for k in range(1, NY)] + [peer("z", k) for k in range(1, NZ)]
    barrier = pltpu.get_barrier_semaphore()
    for device in [after, before] + peers:
        pl.semaphore_signal(barrier, inc=1, device_id=device, device_id_type=MESH)

    own = pltpu.make_async_copy(latent.at[0], window.at[pl.ds(BLOCK, 3 * BLOCK)], local_sem)
    own.start()
    pl.semaphore_wait(barrier, 2 + len(peers))

    def halo_copies(g):
        copies = []
        for part_at in range(2):
            columns = pl.ds(part_at * H * HEAD + g * QUAD, QUAD)
            for side, device in enumerate((after, before)):
                source = 2 * BLOCK if side == 0 else 0
                target = 0 if side == 0 else 4 * BLOCK
                copies.append(
                    pltpu.make_async_remote_copy(
                        src_ref=latent.at[0, pl.ds(source, BLOCK), columns],
                        dst_ref=window.at[pl.ds(target, BLOCK), columns],
                        send_sem=halo_send.at[g, part_at, side],
                        recv_sem=halo_recv.at[g, part_at, side],
                        device_id=device,
                        device_id_type=MESH,
                    )
                )
        return copies

    halos = [halo_copies(g) for g in range(QUADS)]
    for copies in halos:
        for copy in copies:
            copy.start()

    lane = lax.broadcasted_iota(jnp.int32, (1, 2 * BLOCK), 1)
    in_first = lane < BLOCK
    bias = [
        jnp.where(
            in_first,
            slot_bias(blocks, pair_count, region, 0, w, 3 * regions),
            slot_bias(blocks, pair_count, region, 1, w, 3 * regions),
        )
        for w in range(WIN)
    ]
    lane_live = lane < jnp.where(in_first, obs_count[0], BLOCK + obs_count[1])
    row = lax.broadcasted_iota(jnp.int32, (2 * BLOCK, 1), 0)
    row_live = row < jnp.where(row < BLOCK, obs_count[0], BLOCK + obs_count[1])
    head_lane = lax.broadcasted_iota(jnp.int32, (2 * BLOCK, QUAD), 1) // HEAD

    def compute(g):
        columns = pl.ds(g * QUAD, QUAD)
        value_columns = pl.ds(H * HEAD + g * QUAD, QUAD)
        query = queries[:, columns]
        grad = jnp.where(row_live, cotangent[:, columns], 0).astype(BF16)
        query_t, grad_t = query.T, grad.T
        keys, values = window[:, columns], window[:, value_columns]
        keys_t, values_t = keys.T, values.T
        mixed, query_grads = [], []
        key_grads = value_grads = None
        for h in range(HEADS):
            rows = slice(h * HEAD, (h + 1) * HEAD)

            def alone(a):
                pieces = []
                if h > 0:
                    pieces.append(jnp.zeros((h * HEAD, a.shape[1]), a.dtype))
                pieces.append(a[rows])
                if h < HEADS - 1:
                    pieces.append(jnp.zeros(((HEADS - 1 - h) * HEAD, a.shape[1]), a.dtype))
                return jnp.concatenate(pieces, axis=0)

            scores = dot(keys, alone(query_t))
            tops = [
                jnp.max(scores[w * BLOCK : (w + 1) * BLOCK], axis=0, keepdims=True) * (SCALE * LOG2E) + bias[w]
                for w in range(WIN)
            ]
            top = functools.reduce(jnp.maximum, tops)
            shift = jnp.concatenate(
                [jnp.broadcast_to(top - bias[w], (BLOCK, 2 * BLOCK)) for w in range(WIN)], axis=0
            )
            expanded = jnp.exp2(scores * (SCALE * LOG2E) - shift)
            attention = expanded * (1.0 / jnp.sum(expanded, axis=0, keepdims=True))
            attention_low = attention.astype(BF16)
            grad_attention = dot(values, alone(grad_t))
            delta = jnp.sum(attention * grad_attention, axis=0, keepdims=True)
            grad_low = (attention * ((grad_attention - delta) * SCALE)).astype(BF16)
            mixed.append(dot(values_t[rows], attention_low))
            query_grads.append(dot(keys_t[rows], grad_low))
            mine = head_lane == h
            key_part = dot(grad_low, jnp.where(mine, query, 0).astype(BF16))
            value_part = dot(attention_low, jnp.where(mine, grad, 0).astype(BF16))
            key_grads = key_part if key_grads is None else key_grads + key_part
            value_grads = value_part if value_grads is None else value_grads + value_part
        mixed = jnp.where(lane_live, jnp.concatenate(mixed, axis=0), 0.0)
        attended[:, columns] = mixed.T.astype(BF16)
        grad_query[:, columns] = jnp.concatenate(query_grads, axis=0).T.astype(BF16)
        tiles = owner_tiles(key_grads, value_grads)
        rim_out[g, 0] = tiles[:32].astype(BF16)
        middle[g] = tiles[32:128]
        rim_out[g, 1] = tiles[128:].astype(BF16)

    def rim_copies(g):
        return [
            pltpu.make_async_remote_copy(
                src_ref=rim_out.at[g, side],
                dst_ref=rim_in.at[g, side],
                send_sem=rim_send.at[g, side],
                recv_sem=rim_recv.at[g, side],
                device_id=device,
                device_id_type=MESH,
            )
            for side, device in enumerate((before, after))
        ]

    def exchange(axis, source, target, send, recv):
        copies = []
        for k in range(1, NY if axis == "y" else NZ):
            copies.append(
                pltpu.make_async_remote_copy(
                    src_ref=source(along(axis, k)),
                    dst_ref=target(k - 1),
                    send_sem=send(k - 1),
                    recv_sem=recv(k - 1),
                    device_id=peer(axis, k),
                    device_id_type=MESH,
                )
            )
        return copies

    def piece(g, axis, i):
        return part.at[g, i] if axis == "y" else part.at[g, :, i]

    def landing(g, axis, k):
        if axis == "y":
            return first_in.at[g, k, pl.ds(0, NZ)]
        return first_in.at[g, k, pl.ds(0, NY)]

    def first_copies(g):
        axis = FIRST_AXIS[g]
        return exchange(
            axis,
            lambda i: piece(g, axis, i),
            lambda k: landing(g, axis, k),
            lambda k: first_send.at[g, k],
            lambda k: first_recv.at[g, k],
        )

    def second_copies(g):
        axis = "z" if FIRST_AXIS[g] == "y" else "y"
        return exchange(
            axis,
            lambda i: second_out.at[g, i],
            lambda k: second_in.at[g, k],
            lambda k: second_send.at[g, k],
            lambda k: second_recv.at[g, k],
        )

    def start_first(g, rims):
        for copy in rims:
            copy.wait_recv()
        half = part.at[g]
        for i in range(NY):
            owned = middle[g, i * NZ : (i + 1) * NZ]
            for side, start in ((1, 0), (0, 64)):
                low, high = max(i * NZ, start), min((i + 1) * NZ, start + 32)
                if low < high:
                    extra = rim_in[g, side, low - start : high - start].astype(F32)
                    pieces = [extra]
                    if low > i * NZ:
                        pieces.insert(0, jnp.zeros((low - i * NZ, 16, 128), F32))
                    if high < (i + 1) * NZ:
                        pieces.append(jnp.zeros(((i + 1) * NZ - high, 16, 128), F32))
                    owned = owned + jnp.concatenate(pieces, axis=0)
            half[i] = owned.astype(BF16)
        copies = first_copies(g)
        for copy in copies:
            copy.start()
        return copies

    def start_second(g, copies):
        for copy in copies:
            copy.wait_recv()
        axis = FIRST_AXIS[g]
        mine = along(axis, 0)
        total = piece(g, axis, mine)[...].astype(F32)
        for k in range(len(copies)):
            total = total + landing(g, axis, k)[...].astype(F32)
        count = total.shape[0]
        second_out[g, 0:count] = total.astype(BF16)
        copies = second_copies(g)
        for copy in copies:
            copy.start()
        return copies

    def finish(g, copies):
        for copy in copies:
            copy.wait_recv()
        axis = "z" if FIRST_AXIS[g] == "y" else "y"
        total = second_out[g, along(axis, 0)].astype(F32)
        for k in range(len(copies)):
            total = total + second_in[g, k].astype(F32)
        for c in range(4):
            start = (c // 2) * H * HEAD + g * QUAD + (c % 2) * 128
            grad_kv[0, :, start : start + 128] = total[4 * c : 4 * c + 4]

    own.wait()
    rims, firsts, seconds = {}, {}, {}
    for g in range(QUADS):
        for copy in halos[g]:
            copy.wait_recv()
        compute(g)
        rims[g] = rim_copies(g)
        for copy in rims[g]:
            copy.start()
        if g >= 1:
            firsts[g - 1] = start_first(g - 1, rims[g - 1])
        if g >= 2:
            seconds[g - 2] = start_second(g - 2, firsts[g - 2])
    last = QUADS - 1
    firsts[last] = start_first(last, rims[last])
    seconds[last - 1] = start_second(last - 1, firsts[last - 1])
    seconds[last] = start_second(last, firsts[last])
    for g in range(QUADS):
        finish(g, seconds[g])
    for groups in (halos, rims.values(), firsts.values(), seconds.values()):
        for copies in groups:
            for copy in copies:
                copy.wait_send()


def per_device(queries, latent_kv, pair_blocks, pair_count, obs_count, cotangent):
    vmem = pl.BlockSpec(memory_space=pltpu.VMEM)
    smem = pl.BlockSpec(memory_space=pltpu.SMEM)
    hbm = pl.BlockSpec(memory_space=pl.ANY)
    rows, width = queries.shape
    dma = pltpu.SemaphoreType.DMA
    return pl.pallas_call(
        kernel,
        out_shape=(
            jax.ShapeDtypeStruct((rows, width), BF16),
            jax.ShapeDtypeStruct((rows, width), BF16),
            jax.ShapeDtypeStruct((1, 4, 2 * width), F32),
        ),
        in_specs=[vmem, hbm, smem, smem, smem, vmem],
        out_specs=(vmem, vmem, vmem),
        scratch_shapes=[
            pltpu.VMEM((WIN * BLOCK, 2 * width), BF16),
            pltpu.VMEM((QUADS, NY * NZ, 16, 128), F32),
            pltpu.VMEM((QUADS, 2, 32, 16, 128), BF16),
            pltpu.VMEM((QUADS, 2, 32, 16, 128), BF16),
            pltpu.VMEM((QUADS, NY, NZ, 16, 128), BF16),
            pltpu.VMEM((QUADS, NZ - 1, NZ, 16, 128), BF16),
            pltpu.VMEM((QUADS, NZ, 16, 128), BF16),
            pltpu.VMEM((QUADS, NZ - 1, 16, 128), BF16),
            dma,
            dma((QUADS, 2, 2)),
            dma((QUADS, 2, 2)),
            dma((QUADS, 2)),
            dma((QUADS, 2)),
            dma((QUADS, NZ - 1)),
            dma((QUADS, NZ - 1)),
            dma((QUADS, NZ - 1)),
            dma((QUADS, NZ - 1)),
        ],
        compiler_params=pltpu.CompilerParams(
            collective_id=0, has_side_effects=True, vmem_limit_bytes=56 * 1024 * 1024
        ),
    )(queries, latent_kv, pair_blocks, pair_count, obs_count, cotangent)


def solution(mesh):
    placed = (
        P(("obs", "grid"), None),
        P("grid", None, None),
        P(("obs", "grid"), None),
        P(("obs", "grid")),
        P(("obs", "grid")),
        P(("obs", "grid"), None),
    )
    return jax.shard_map(
        per_device,
        mesh=mesh,
        in_specs=placed,
        out_specs=(P(("obs", "grid"), None), P(("obs", "grid"), None), P("grid", "obs", None)),
        check_vma=False,
    )
```

```python
import functools
import math

import jax
import jax.numpy as jnp
from jax import lax
from jax.experimental import pallas as pl
from jax.experimental.pallas import tpu as pltpu
from jax.sharding import PartitionSpec as P

H = 16
HEAD = 64
NY, NZ = 8, 12
BLOCK = 128
WIN = 5
QUADS = 4
HEADS = H // QUADS
QUAD = HEADS * HEAD
MESH = pl.DeviceIdType.MESH
SCALE = 1.0 / math.sqrt(HEAD)
LOG2E = 1.4426950408889634
F32, BF16 = jnp.float32, jnp.bfloat16
FIRST_AXIS = ("z", "y", "y", "y")
RUNS = {
    "y": ((1, 4, 3), (1, 2, 1), (-1, 3, 2), (-1, 1, 1)),
    "z": ((1, 6, 5), (1, 4, 3), (1, 2, 1), (-1, 5, 4), (-1, 3, 2), (-1, 1, 1)),
}


def dot(a, b):
    return jnp.dot(a, b, preferred_element_type=F32)


def slot_bias(blocks_ref, count_ref, region, n, w, total):
    wanted = lax.rem(3 * region - 1 + w + total, total)
    uses = 0
    for p in range(blocks_ref.shape[1]):
        live = (blocks_ref[n, p] == wanted) & (p < count_ref[n])
        uses = uses + jnp.where(live, 1, 0)
    return jnp.where(
        uses == 0,
        F32(-1e30),
        jnp.where(
            uses == 1,
            F32(0.0),
            jnp.where(uses == 2, F32(1.0), jnp.where(uses == 3, F32(math.log2(3.0)), F32(2.0))),
        ),
    )


def owner_tiles(keys, values):
    rows = keys.shape[0]
    low = lax.broadcasted_iota(jnp.int32, (rows // 8, 8, 128), 1) < 4

    def split(a, lane):
        return a[:, lane : lane + 128].reshape(rows // 8, 8, 128)

    def pair(a):
        left, right = split(a, 0), split(a, 128)
        even = jnp.where(low, left, pltpu.roll(right, 4, 1))
        odd = jnp.where(low, pltpu.roll(left, 4, 1), right)
        return even, odd

    key_even, key_odd = pair(keys)
    value_even, value_odd = pair(values)
    even = jnp.concatenate([key_even, value_even], axis=1)
    odd = jnp.concatenate([key_odd, value_odd], axis=1)
    return jnp.stack([even, odd], axis=1).reshape(rows // 4, 16, 128)


def kernel(
    queries, latent, blocks, pair_count, obs_count, cotangent,
    attended, grad_query, grad_kv,
    query_in, grad_in, lows, grad_lows, window, middle, rim_out, rim_in, part, first_in, hop_out, second_out, second_in,
    local_sem, halo_send, halo_recv, rim_send, rim_recv,
    first_send, first_recv, second_send, second_recv,
):
    place, region = lax.axis_index("obs"), lax.axis_index("grid")
    regions = lax.axis_size("grid")
    y, z = place // NZ, lax.rem(place, NZ)
    after = (place, lax.rem(region + 1, regions))
    before = (place, lax.rem(region + regions - 1, regions))

    def along(axis, k):
        if axis == "y":
            return lax.rem(y + k + NY, NY)
        return lax.rem(z + k + NZ, NZ)

    def peer(axis, k):
        if axis == "y":
            return (along(axis, k) * NZ + z, region)
        return (y * NZ + along(axis, k), region)

    peers = [peer("y", k) for k in range(1, NY)] + [peer("z", k) for k in range(1, NZ)]
    barrier = pltpu.get_barrier_semaphore()
    for device in [after, before] + peers:
        pl.semaphore_signal(barrier, inc=1, device_id=device, device_id_type=MESH)

    loads = [
        pltpu.make_async_copy(latent.at[0], window.at[pl.ds(BLOCK, 3 * BLOCK)], local_sem.at[0]),
        pltpu.make_async_copy(queries, query_in, local_sem.at[1]),
        pltpu.make_async_copy(cotangent, grad_in, local_sem.at[2]),
    ]
    for copy in loads:
        copy.start()
    pl.semaphore_wait(barrier, 2 + len(peers))

    def halo_copies(g):
        copies = []
        for part_at in range(2):
            columns = pl.ds(part_at * H * HEAD + g * QUAD, QUAD)
            for side, device in enumerate((after, before)):
                source = 2 * BLOCK if side == 0 else 0
                target = 0 if side == 0 else 4 * BLOCK
                copies.append(
                    pltpu.make_async_remote_copy(
                        src_ref=latent.at[0, pl.ds(source, BLOCK), columns],
                        dst_ref=window.at[pl.ds(target, BLOCK), columns],
                        send_sem=halo_send.at[g, part_at, side],
                        recv_sem=halo_recv.at[g, part_at, side],
                        device_id=device,
                        device_id_type=MESH,
                    )
                )
        return copies

    halos = [halo_copies(g) for g in range(QUADS)]
    for copies in halos:
        for copy in copies:
            copy.start()

    lane = lax.broadcasted_iota(jnp.int32, (1, 2 * BLOCK), 1)
    in_first = lane < BLOCK
    bias = [
        jnp.where(
            in_first,
            slot_bias(blocks, pair_count, region, 0, w, 3 * regions),
            slot_bias(blocks, pair_count, region, 1, w, 3 * regions),
        )
        for w in range(WIN)
    ]
    lane_live = lane < jnp.where(in_first, obs_count[0], BLOCK + obs_count[1])
    row = lax.broadcasted_iota(jnp.int32, (2 * BLOCK, 1), 0)
    row_live = row < jnp.where(row < BLOCK, obs_count[0], BLOCK + obs_count[1])
    head_lane = lax.broadcasted_iota(jnp.int32, (2 * BLOCK, QUAD), 1) // HEAD

    def compute(g):
        columns = pl.ds(g * QUAD, QUAD)
        value_columns = pl.ds(H * HEAD + g * QUAD, QUAD)
        query = query_in[:, columns]
        grad = jnp.where(row_live, grad_in[:, columns], 0).astype(BF16)
        query_t, grad_t = query.T, grad.T
        keys, values = window[:, columns], window[:, value_columns]
        def alone(a, h):
            rows = slice(h * HEAD, (h + 1) * HEAD)
            pieces = []
            if h > 0:
                pieces.append(jnp.zeros((h * HEAD, a.shape[1]), a.dtype))
            pieces.append(a[rows])
            if h < HEADS - 1:
                pieces.append(jnp.zeros(((HEADS - 1 - h) * HEAD, a.shape[1]), a.dtype))
            return jnp.concatenate(pieces, axis=0)

        def front(h):
            return dot(keys, alone(query_t, h)), dot(values, alone(grad_t, h))

        ready = front(0)
        for h in range(HEADS):
            scores, grad_attention = ready
            if h < HEADS - 1:
                ready = front(h + 1)
            tops = [
                jnp.max(scores[w * BLOCK : (w + 1) * BLOCK], axis=0, keepdims=True) * (SCALE * LOG2E) + bias[w]
                for w in range(WIN)
            ]
            top = functools.reduce(jnp.maximum, tops)
            shift = jnp.concatenate(
                [jnp.broadcast_to(top - bias[w], (BLOCK, 2 * BLOCK)) for w in range(WIN)], axis=0
            )
            expanded = jnp.exp2(scores * (SCALE * LOG2E) - shift)
            attention = expanded * (1.0 / jnp.sum(expanded, axis=0, keepdims=True))
            attention_low = attention.astype(BF16)
            delta = jnp.sum(attention * grad_attention, axis=0, keepdims=True)
            grad_low = (attention * ((grad_attention - delta) * SCALE)).astype(BF16)
            lows[g * HEADS + h] = attention_low
            grad_lows[g * HEADS + h] = grad_low

        def spread(a):
            return jnp.concatenate([jnp.where(head_lane == h, a, 0).astype(BF16) for h in range(HEADS)], axis=0)

        query_spread, grad_spread = spread(query), spread(grad)

        def grad_tiles(start, count):
            at = slice(start * BLOCK, (start + count) * BLOCK)

            def heads(ref):
                return jnp.concatenate([ref[g * HEADS + h, at] for h in range(HEADS)], axis=1)

            return owner_tiles(dot(heads(grad_lows), query_spread), dot(heads(lows), grad_spread))

        rim_out[g, 0] = grad_tiles(0, 1).astype(BF16)
        rim_out[g, 1] = grad_tiles(4, 1).astype(BF16)
        rims[g] = rim_copies(g)
        for copy in rims[g]:
            copy.start()
        middle[g] = grad_tiles(1, 3)

    def hand_over(g):
        columns = pl.ds(g * QUAD, QUAD)
        keys_t = window[:, columns].T
        values_t = window[:, pl.ds(H * HEAD + g * QUAD, QUAD)].T
        mixed, query_grads = [], []
        for h in range(HEADS):
            rows = slice(h * HEAD, (h + 1) * HEAD)
            mixed.append(dot(values_t[rows], lows[g * HEADS + h]))
            query_grads.append(dot(keys_t[rows], grad_lows[g * HEADS + h]))
        mixed = jnp.where(lane_live, jnp.concatenate(mixed, axis=0), 0.0)
        attended[:, columns] = mixed.T.astype(BF16)
        grad_query[:, columns] = jnp.concatenate(query_grads, axis=0).T.astype(BF16)

    def rim_copies(g):
        return [
            pltpu.make_async_remote_copy(
                src_ref=rim_out.at[g, side],
                dst_ref=rim_in.at[g, side],
                send_sem=rim_send.at[g, side],
                recv_sem=rim_recv.at[g, side],
                device_id=device,
                device_id_type=MESH,
            )
            for side, device in enumerate((before, after))
        ]

    def exchange(axis, source, target, send, recv):
        copies = []
        size = NY if axis == "y" else NZ
        for k in sorted(range(1, size), key=lambda k: -min(k, size - k)):
            copies.append(
                pltpu.make_async_remote_copy(
                    src_ref=source(along(axis, k)),
                    dst_ref=target(k - 1),
                    send_sem=send(k - 1),
                    recv_sem=recv(k - 1),
                    device_id=peer(axis, k),
                    device_id_type=MESH,
                )
            )
        return copies

    def piece(g, axis, i):
        return part.at[g, i] if axis == "y" else part.at[g, :, i]

    def landing(g, axis, k):
        if axis == "y":
            return first_in.at[g, k, pl.ds(0, NZ)]
        return first_in.at[g, k, pl.ds(0, NY)]

    def first_copy(g, axis, source, k, slot):
        return pltpu.make_async_remote_copy(
            src_ref=source,
            dst_ref=landing(g, axis, slot),
            send_sem=first_send.at[g, slot],
            recv_sem=first_recv.at[g, slot],
            device_id=peer(axis, k),
            device_id_type=MESH,
        )

    def runs_of(g):
        axis, turn = FIRST_AXIS[g], 1 if g % 2 else -1
        runs = [(turn * sign, far, near) for sign, far, near in RUNS[axis]]
        pairs = [run for run in runs if run[1] != run[2]]
        return axis, pairs, [run for run in runs if run[1] == run[2]]

    def second_copies(g):
        axis = "z" if FIRST_AXIS[g] == "y" else "y"
        return exchange(
            axis,
            lambda i: second_out.at[g, i],
            lambda k: second_in.at[g, k],
            lambda k: second_send.at[g, k],
            lambda k: second_recv.at[g, k],
        )

    def start_first(g, rims):
        for copy in rims:
            copy.wait_recv()
        half = part.at[g]
        for i in range(NY):
            owned = middle[g, i * NZ : (i + 1) * NZ]
            for side, start in ((1, 0), (0, 64)):
                low, high = max(i * NZ, start), min((i + 1) * NZ, start + 32)
                if low < high:
                    extra = rim_in[g, side, low - start : high - start].astype(F32)
                    pieces = [extra]
                    if low > i * NZ:
                        pieces.insert(0, jnp.zeros((low - i * NZ, 16, 128), F32))
                    if high < (i + 1) * NZ:
                        pieces.append(jnp.zeros(((i + 1) * NZ - high, 16, 128), F32))
                    owned = owned + jnp.concatenate(pieces, axis=0)
            half[i] = owned.astype(BF16)
        axis, pairs, singles = runs_of(g)
        copies = []
        for slot, (sign, far, _) in enumerate(pairs):
            copies.append(first_copy(g, axis, piece(g, axis, along(axis, sign * far)), sign, slot))
        for slot, (sign, near, _) in enumerate(singles):
            at = sign * near
            slot += 2 * len(pairs)
            copies.append(first_copy(g, axis, piece(g, axis, along(axis, at)), at, slot))
        for copy in copies:
            copy.start()
        return copies

    def pass_on(g, copies):
        axis, pairs, _ = runs_of(g)
        count = NZ if axis == "y" else NY
        sent = []
        for slot, (sign, _, near) in enumerate(pairs):
            copies[slot].wait_recv()
            own_term = piece(g, axis, along(axis, sign * near))[...].astype(F32)
            total = own_term + landing(g, axis, slot)[...].astype(F32)
            staged = hop_out.at[g, slot, pl.ds(0, count)]
            staged[...] = total.astype(BF16)
            copy = first_copy(g, axis, staged, sign * near, len(pairs) + slot)
            copy.start()
            sent.append(copy)
        return sent + copies[len(pairs) :], copies[: len(pairs)]

    def start_second(g, copies):
        for copy in copies:
            copy.wait_recv()
        axis, pairs, _ = runs_of(g)
        mine = along(axis, 0)
        total = piece(g, axis, mine)[...].astype(F32)
        for k in range(len(copies)):
            total = total + landing(g, axis, len(pairs) + k)[...].astype(F32)
        count = total.shape[0]
        second_out[g, 0:count] = total.astype(BF16)
        copies = second_copies(g)
        for copy in copies:
            copy.start()
        return copies

    def finish(g, copies):
        for copy in copies:
            copy.wait_recv()
        axis = "z" if FIRST_AXIS[g] == "y" else "y"
        total = second_out[g, along(axis, 0)].astype(F32)
        for k in range(len(copies)):
            total = total + second_in[g, k].astype(F32)
        for c in range(4):
            start = (c // 2) * H * HEAD + g * QUAD + (c % 2) * 128
            grad_kv[0, :, start : start + 128] = total[4 * c : 4 * c + 4]

    for copy in loads:
        copy.wait()
    rims, firsts, finals, passed, seconds = {}, {}, {}, {}, {}

    def front(g):
        for copy in halos[g]:
            copy.wait_recv()
        compute(g)

    def first(g):
        firsts[g] = start_first(g, rims[g])

    def passing(g):
        finals[g], passed[g] = pass_on(g, firsts[g])

    def second(g):
        seconds[g] = start_second(g, finals[g])

    plan = (
        (front, 0), (front, 1), (front, 2), (first, 0), (front, 3), (first, 1), (hand_over, 0),
        (first, 2), (passing, 0), (hand_over, 1), (first, 3), (passing, 1), (hand_over, 2),
        (passing, 2), (hand_over, 3), (passing, 3), (second, 0), (second, 1), (second, 2),
        (second, 3),
    )
    for step, g in plan:
        step(g)
    for g in range(QUADS):
        finish(g, seconds[g])
    for groups in (halos, rims.values(), finals.values(), passed.values(), seconds.values()):
        for copies in groups:
            for copy in copies:
                copy.wait_send()


def hand_out(*refs):
    for source, target in zip(refs[:3], refs[3:], strict=True):
        target[...] = source[...]


def per_device(queries, latent_kv, pair_blocks, pair_count, obs_count, cotangent):
    vmem = pl.BlockSpec(memory_space=pltpu.VMEM)
    smem = pl.BlockSpec(memory_space=pltpu.SMEM)
    hbm = pl.BlockSpec(memory_space=pl.ANY)
    rows, width = queries.shape
    dma = pltpu.SemaphoreType.DMA
    results = pl.pallas_call(
        kernel,
        out_shape=(
            jax.ShapeDtypeStruct((rows, width), BF16),
            jax.ShapeDtypeStruct((rows, width), BF16),
            jax.ShapeDtypeStruct((1, 4, 2 * width), F32),
        ),
        in_specs=[hbm, hbm, smem, smem, smem, hbm],
        out_specs=(vmem, vmem, vmem),
        scratch_shapes=[
            pltpu.VMEM((rows, width), BF16),
            pltpu.VMEM((rows, width), BF16),
            pltpu.VMEM((H, WIN * BLOCK, rows), BF16),
            pltpu.VMEM((H, WIN * BLOCK, rows), BF16),
            pltpu.VMEM((WIN * BLOCK, 2 * width), BF16),
            pltpu.VMEM((QUADS, NY * NZ, 16, 128), F32),
            pltpu.VMEM((QUADS, 2, 32, 16, 128), BF16),
            pltpu.VMEM((QUADS, 2, 32, 16, 128), BF16),
            pltpu.VMEM((QUADS, NY, NZ, 16, 128), BF16),
            pltpu.VMEM((QUADS, NZ - 1, NZ, 16, 128), BF16),
            pltpu.VMEM((QUADS, 5, NZ, 16, 128), BF16),
            pltpu.VMEM((QUADS, NZ, 16, 128), BF16),
            pltpu.VMEM((QUADS, NZ - 1, 16, 128), BF16),
            dma((3,)),
            dma((QUADS, 2, 2)),
            dma((QUADS, 2, 2)),
            dma((QUADS, 2)),
            dma((QUADS, 2)),
            dma((QUADS, NZ - 1)),
            dma((QUADS, NZ - 1)),
            dma((QUADS, NZ - 1)),
            dma((QUADS, NZ - 1)),
        ],
        compiler_params=pltpu.CompilerParams(
            collective_id=0, has_side_effects=True, vmem_limit_bytes=56 * 1024 * 1024
        ),
    )(queries, latent_kv, pair_blocks, pair_count, obs_count, cotangent)
    return pl.pallas_call(
        hand_out,
        out_shape=tuple(jax.ShapeDtypeStruct(r.shape, r.dtype) for r in results),
        in_specs=[vmem] * 3,
        out_specs=(vmem,) * 3,
    )(*results)


def solution(mesh):
    placed = (
        P(("obs", "grid"), None),
        P("grid", None, None),
        P(("obs", "grid"), None),
        P(("obs", "grid")),
        P(("obs", "grid")),
        P(("obs", "grid"), None),
    )
    return jax.shard_map(
        per_device,
        mesh=mesh,
        in_specs=placed,
        out_specs=(P(("obs", "grid"), None), P(("obs", "grid"), None), P("grid", "obs", None)),
        check_vma=False,
    )
```

```python
import functools
import math

import jax
import jax.numpy as jnp
from jax import lax
from jax.experimental import pallas as pl
from jax.experimental.pallas import tpu as pltpu
from jax.sharding import PartitionSpec as P

H = 16
HEAD = 64
NY, NZ = 8, 12
BLOCK = 128
WIN = 5
QUADS = 4
HEADS = H // QUADS
QUAD = HEADS * HEAD
MESH = pl.DeviceIdType.MESH
SCALE = 1.0 / math.sqrt(HEAD)
LOG2E = 1.4426950408889634
F32, BF16 = jnp.float32, jnp.bfloat16
HALO_QUADS = ((0, 1), (1, 1), (2, 2))
FIRST_AXIS = ("z", "y", "z", "y")
RUNS = {
    "y": ((1, 4, 3), (1, 2, 1), (-1, 3, 2), (-1, 1, 1)),
    "z": ((1, 6, 5), (1, 4, 3), (1, 2, 1), (-1, 5, 4), (-1, 3, 2), (-1, 1, 1)),
}


def dot(a, b):
    return jnp.dot(a, b, preferred_element_type=F32)


def slot_bias(blocks_ref, count_ref, region, n, w, total):
    wanted = lax.rem(3 * region - 1 + w + total, total)
    uses = 0
    for p in range(blocks_ref.shape[1]):
        live = (blocks_ref[n, p] == wanted) & (p < count_ref[n])
        uses = uses + jnp.where(live, 1, 0)
    return jnp.where(
        uses == 0,
        F32(-1e30),
        jnp.where(
            uses == 1,
            F32(0.0),
            jnp.where(uses == 2, F32(1.0), jnp.where(uses == 3, F32(math.log2(3.0)), F32(2.0))),
        ),
    )


def owner_tiles(keys, values):
    rows = keys.shape[0]
    low = lax.broadcasted_iota(jnp.int32, (rows // 8, 8, 128), 1) < 4

    def split(a, lane):
        return a[:, lane : lane + 128].reshape(rows // 8, 8, 128)

    def pair(a):
        left, right = split(a, 0), split(a, 128)
        even = jnp.where(low, left, pltpu.roll(right, 4, 1))
        odd = jnp.where(low, pltpu.roll(left, 4, 1), right)
        return even, odd

    key_even, key_odd = pair(keys)
    value_even, value_odd = pair(values)
    even = jnp.concatenate([key_even, value_even], axis=1)
    odd = jnp.concatenate([key_odd, value_odd], axis=1)
    return jnp.stack([even, odd], axis=1).reshape(rows // 4, 16, 128)


def kernel(
    queries, latent, blocks, pair_count, obs_count, cotangent,
    attended, grad_query, grad_kv,
    query_in, grad_in, mixed_out, query_grad_out, lows, grad_lows, window, middle,
    rim_out, rim_in, part, first_in, hop_out, second_out, second_in,
    local_sem, store_sem, halo_send, halo_recv, rim_send, rim_recv,
    first_send, first_recv, second_send, second_recv,
):
    place, region = lax.axis_index("obs"), lax.axis_index("grid")
    regions = lax.axis_size("grid")
    y, z = place // NZ, lax.rem(place, NZ)
    after = (place, lax.rem(region + 1, regions))
    before = (place, lax.rem(region + regions - 1, regions))

    def around(at, k, size):
        moved = at + k % size
        return jnp.where(moved >= size, moved - size, moved)

    at_y = [around(y, k, NY) for k in range(NY)]
    at_z = [around(z, k, NZ) for k in range(NZ)]
    place_y = [i * NZ + z for i in at_y]
    place_z = [y * NZ + i for i in at_z]

    def along(axis, k):
        return at_y[k % NY] if axis == "y" else at_z[k % NZ]

    def peer(axis, k):
        return (place_y[k % NY] if axis == "y" else place_z[k % NZ], region)

    peers = [peer("y", k) for k in range(1, NY)] + [peer("z", k) for k in range(1, NZ)]
    barrier = pltpu.get_barrier_semaphore()
    for device in [after, before] + peers:
        pl.semaphore_signal(barrier, inc=1, device_id=device, device_id_type=MESH)

    loads = [
        pltpu.make_async_copy(latent.at[0], window.at[pl.ds(BLOCK, 3 * BLOCK)], local_sem.at[0]),
        pltpu.make_async_copy(queries, query_in, local_sem.at[1]),
        pltpu.make_async_copy(cotangent, grad_in, local_sem.at[2]),
    ]
    for copy in loads:
        copy.start()
    pl.semaphore_wait(barrier, 2 + len(peers))

    def halo_copies(g):
        copies = []
        first_quad, count = HALO_QUADS[g]
        for part_at in range(2):
            columns = pl.ds(part_at * H * HEAD + first_quad * QUAD, count * QUAD)
            for side, device in enumerate((after, before)):
                source = 2 * BLOCK if side == 0 else 0
                target = 0 if side == 0 else 4 * BLOCK
                copies.append(
                    pltpu.make_async_remote_copy(
                        src_ref=latent.at[0, pl.ds(source, BLOCK), columns],
                        dst_ref=window.at[pl.ds(target, BLOCK), columns],
                        send_sem=halo_send.at[g, part_at, side],
                        recv_sem=halo_recv.at[g, part_at, side],
                        device_id=device,
                        device_id_type=MESH,
                    )
                )
        return copies

    halos = [halo_copies(g) for g in range(len(HALO_QUADS))]
    for copies in halos:
        for copy in copies:
            copy.start()

    lane = lax.broadcasted_iota(jnp.int32, (1, 2 * BLOCK), 1)
    in_first = lane < BLOCK
    bias = [
        jnp.where(
            in_first,
            slot_bias(blocks, pair_count, region, 0, w, 3 * regions),
            slot_bias(blocks, pair_count, region, 1, w, 3 * regions),
        )
        for w in range(WIN)
    ]
    lane_live = lane < jnp.where(in_first, obs_count[0], BLOCK + obs_count[1])
    row = lax.broadcasted_iota(jnp.int32, (2 * BLOCK, 1), 0)
    row_live = row < jnp.where(row < BLOCK, obs_count[0], BLOCK + obs_count[1])
    head_lane = lax.broadcasted_iota(jnp.int32, (2 * BLOCK, QUAD), 1) // HEAD

    def compute(g):
        columns = pl.ds(g * QUAD, QUAD)
        value_columns = pl.ds(H * HEAD + g * QUAD, QUAD)
        query = query_in[:, columns]
        grad = jnp.where(row_live, grad_in[:, columns], 0).astype(BF16)
        query_t, grad_t = query.T, grad.T
        keys, values = window[:, columns], window[:, value_columns]
        def alone(a, h):
            rows = slice(h * HEAD, (h + 1) * HEAD)
            pieces = []
            if h > 0:
                pieces.append(jnp.zeros((h * HEAD, a.shape[1]), a.dtype))
            pieces.append(a[rows])
            if h < HEADS - 1:
                pieces.append(jnp.zeros(((HEADS - 1 - h) * HEAD, a.shape[1]), a.dtype))
            return jnp.concatenate(pieces, axis=0)

        def front(h):
            return dot(keys, alone(query_t, h)), dot(values, alone(grad_t, h))

        ready = front(0)
        for h in range(HEADS):
            scores, grad_attention = ready
            if h < HEADS - 1:
                ready = front(h + 1)
            tops = [
                jnp.max(scores[w * BLOCK : (w + 1) * BLOCK], axis=0, keepdims=True) * (SCALE * LOG2E) + bias[w]
                for w in range(WIN)
            ]
            top = functools.reduce(jnp.maximum, tops)
            shift = jnp.concatenate(
                [jnp.broadcast_to(top - bias[w], (BLOCK, 2 * BLOCK)) for w in range(WIN)], axis=0
            )
            expanded = jnp.exp2(scores * (SCALE * LOG2E) - shift)
            attention = expanded * (1.0 / jnp.sum(expanded, axis=0, keepdims=True))
            attention_low = attention.astype(BF16)
            delta = jnp.sum(attention * grad_attention, axis=0, keepdims=True)
            grad_low = (attention * ((grad_attention - delta) * SCALE)).astype(BF16)
            lows[g * HEADS + h] = attention_low
            grad_lows[g * HEADS + h] = grad_low

        def spread(a):
            return jnp.concatenate([jnp.where(head_lane == h, a, 0).astype(BF16) for h in range(HEADS)], axis=0)

        query_spread, grad_spread = spread(query), spread(grad)

        def grad_tiles(start, count):
            at = slice(start * BLOCK, (start + count) * BLOCK)

            def heads(ref):
                return jnp.concatenate([ref[g * HEADS + h, at] for h in range(HEADS)], axis=1)

            return owner_tiles(dot(heads(grad_lows), query_spread), dot(heads(lows), grad_spread))

        rim_out[g, 0] = grad_tiles(0, 1).astype(BF16)
        rim_out[g, 1] = grad_tiles(4, 1).astype(BF16)
        rims[g] = rim_copies(g)
        for copy in rims[g]:
            copy.start()
        middle[g] = grad_tiles(1, 3)

    def hand_over(g):
        columns = pl.ds(g * QUAD, QUAD)
        keys_t = window[:, columns].T
        values_t = window[:, pl.ds(H * HEAD + g * QUAD, QUAD)].T
        mixed, query_grads = [], []
        for h in range(HEADS):
            rows = slice(h * HEAD, (h + 1) * HEAD)
            mixed.append(dot(values_t[rows], lows[g * HEADS + h]))
            query_grads.append(dot(keys_t[rows], grad_lows[g * HEADS + h]))
        mixed = jnp.where(lane_live, jnp.concatenate(mixed, axis=0), 0.0)
        mixed_out[:, columns] = mixed.T.astype(BF16)
        query_grad_out[:, columns] = jnp.concatenate(query_grads, axis=0).T.astype(BF16)
        for i, (held, result) in enumerate(((mixed_out, attended), (query_grad_out, grad_query))):
            copy = pltpu.make_async_copy(held.at[:, columns], result.at[:, columns], store_sem.at[g, i])
            copy.start()
            stores.append(copy)

    def rim_copies(g):
        return [
            pltpu.make_async_remote_copy(
                src_ref=rim_out.at[g, side],
                dst_ref=rim_in.at[g, side],
                send_sem=rim_send.at[g, side],
                recv_sem=rim_recv.at[g, side],
                device_id=device,
                device_id_type=MESH,
            )
            for side, device in enumerate((before, after))
        ]

    def exchange(axis, source, target, send, recv):
        copies = []
        size = NY if axis == "y" else NZ
        for k in sorted(range(1, size), key=lambda k: -min(k, size - k)):
            copies.append(
                pltpu.make_async_remote_copy(
                    src_ref=source(along(axis, k)),
                    dst_ref=target(k - 1),
                    send_sem=send(k - 1),
                    recv_sem=recv(k - 1),
                    device_id=peer(axis, k),
                    device_id_type=MESH,
                )
            )
        return copies

    def piece(g, axis, i):
        return part.at[g, i] if axis == "y" else part.at[g, :, i]

    def landing(g, axis, k):
        if axis == "y":
            return first_in.at[g, k, pl.ds(0, NZ)]
        return first_in.at[g, k, pl.ds(0, NY)]

    def first_copy(g, axis, source, k, slot):
        return pltpu.make_async_remote_copy(
            src_ref=source,
            dst_ref=landing(g, axis, slot),
            send_sem=first_send.at[g, slot],
            recv_sem=first_recv.at[g, slot],
            device_id=peer(axis, k),
            device_id_type=MESH,
        )

    def runs_of(g):
        axis, turn = FIRST_AXIS[g], 1 if g < QUADS // 2 else -1
        runs, at = [], 0
        hops = sum(far - near for _, far, near in RUNS[axis])
        for n, (sign, far, near) in enumerate(RUNS[axis]):
            runs.append((turn * sign, tuple(range(far, near - 1, -1)), at, hops + n))
            at += far - near
        return axis, runs, hops

    def send_step(g, step, source_of):
        axis, runs, _ = runs_of(g)
        for run, (sign, distances, at, last) in enumerate(runs):
            if step >= len(distances):
                continue
            source = source_of(axis, run, sign * distances[step], at + step - 1)
            if step == len(distances) - 1:
                copy = first_copy(g, axis, source, sign * distances[step], last)
            else:
                copy = first_copy(g, axis, source, sign, at + step)
            copy.start()
            firsts[g][last if step == len(distances) - 1 else at + step] = copy

    def second_copies(g):
        axis = "z" if FIRST_AXIS[g] == "y" else "y"
        return exchange(
            axis,
            lambda i: second_out.at[g, i],
            lambda k: second_in.at[g, k],
            lambda k: second_send.at[g, k],
            lambda k: second_recv.at[g, k],
        )

    def start_first(g, rims):
        for copy in rims:
            copy.wait_recv()
        half = part.at[g]
        for i in range(NY):
            owned = middle[g, i * NZ : (i + 1) * NZ]
            for side, start in ((1, 0), (0, 64)):
                low, high = max(i * NZ, start), min((i + 1) * NZ, start + 32)
                if low < high:
                    extra = rim_in[g, side, low - start : high - start].astype(F32)
                    pieces = [extra]
                    if low > i * NZ:
                        pieces.insert(0, jnp.zeros((low - i * NZ, 16, 128), F32))
                    if high < (i + 1) * NZ:
                        pieces.append(jnp.zeros(((i + 1) * NZ - high, 16, 128), F32))
                    owned = owned + jnp.concatenate(pieces, axis=0)
            half[i] = owned.astype(BF16)
        firsts[g] = {}
        send_step(g, 0, lambda axis, run, at, slot: piece(g, axis, along(axis, at)))

    def pass_on(g, step):
        def source_of(axis, run, at, slot):
            firsts[g][slot].wait_recv()
            total = piece(g, axis, along(axis, at))[...].astype(F32) + landing(g, axis, slot)[...].astype(F32)
            staged = hop_out.at[g, slot, pl.ds(0, total.shape[0])]
            staged[...] = total.astype(BF16)
            return staged

        send_step(g, step, source_of)

    def start_second(g):
        axis, runs, hops = runs_of(g)
        mine = along(axis, 0)
        total = piece(g, axis, mine)[...].astype(F32)
        for k in range(hops, hops + len(runs)):
            firsts[g][k].wait_recv()
            total = total + landing(g, axis, k)[...].astype(F32)
        count = total.shape[0]
        second_out[g, 0:count] = total.astype(BF16)
        copies = second_copies(g)
        for copy in copies:
            copy.start()
        return copies

    def finish(g, copies):
        for copy in copies:
            copy.wait_recv()
        axis = "z" if FIRST_AXIS[g] == "y" else "y"
        total = second_out[g, along(axis, 0)].astype(F32)
        for k in range(len(copies)):
            total = total + second_in[g, k].astype(F32)
        for c in range(4):
            start = (c // 2) * H * HEAD + g * QUAD + (c % 2) * 128
            grad_kv[0, :, start : start + 128] = total[4 * c : 4 * c + 4]

    for copy in loads:
        copy.wait()
    rims, firsts, seconds, stores = {}, {}, {}, []

    def front(g):
        if g < len(HALO_QUADS):
            for copy in halos[g]:
                copy.wait_recv()
        compute(g)

    def first(g):
        start_first(g, rims[g])

    def second(g):
        seconds[g] = start_second(g)

    plan = (
        (front, 0), (front, 1), (front, 2), (first, 0), (front, 3), (first, 1), (hand_over, 0), (first, 2), (pass_on, 0, 1), (hand_over, 1), (first, 3), (pass_on, 1, 1), (hand_over, 2),
        (pass_on, 2, 1), (hand_over, 3), (pass_on, 3, 1), (second, 0), (second, 1), (second, 2), (second, 3),
    )
    for step, *at in plan:
        step(*at)
    for g in range(QUADS):
        finish(g, seconds[g])
    for copy in stores:
        copy.wait()
    hops = [list(copies.values()) for copies in firsts.values()]
    for groups in (halos, rims.values(), hops, seconds.values()):
        for copies in groups:
            for copy in copies:
                copy.wait_send()


def hand_out(*refs):
    sources, targets, held, sems = refs[:3], refs[3:6], refs[6:9], refs[9]
    loads = [pltpu.make_async_copy(a, b, sems.at[0, i]) for i, (a, b) in enumerate(zip(sources, held))]
    stores = [pltpu.make_async_copy(a, b, sems.at[1, i]) for i, (a, b) in enumerate(zip(held, targets))]
    for copy in loads:
        copy.start()
    for load, store in zip(loads, stores):
        load.wait()
        store.start()
    for copy in stores:
        copy.wait()


def per_device(queries, latent_kv, pair_blocks, pair_count, obs_count, cotangent):
    vmem = pl.BlockSpec(memory_space=pltpu.VMEM)
    smem = pl.BlockSpec(memory_space=pltpu.SMEM)
    hbm = pl.BlockSpec(memory_space=pl.ANY)
    rows, width = queries.shape
    dma = pltpu.SemaphoreType.DMA
    results = pl.pallas_call(
        kernel,
        out_shape=(
            jax.ShapeDtypeStruct((rows, width), BF16),
            jax.ShapeDtypeStruct((rows, width), BF16),
            jax.ShapeDtypeStruct((1, 4, 2 * width), F32),
        ),
        in_specs=[hbm, hbm, smem, smem, smem, hbm],
        out_specs=(hbm, hbm, vmem),
        scratch_shapes=[
            pltpu.VMEM((rows, width), BF16),
            pltpu.VMEM((rows, width), BF16),
            pltpu.VMEM((rows, width), BF16),
            pltpu.VMEM((rows, width), BF16),
            pltpu.VMEM((H, WIN * BLOCK, rows), BF16),
            pltpu.VMEM((H, WIN * BLOCK, rows), BF16),
            pltpu.VMEM((WIN * BLOCK, 2 * width), BF16),
            pltpu.VMEM((QUADS, NY * NZ, 16, 128), F32),
            pltpu.VMEM((QUADS, 2, 32, 16, 128), BF16),
            pltpu.VMEM((QUADS, 2, 32, 16, 128), BF16),
            pltpu.VMEM((QUADS, NY, NZ, 16, 128), BF16),
            pltpu.VMEM((QUADS, NZ - 1, NZ, 16, 128), BF16),
            pltpu.VMEM((QUADS, NZ, NZ, 16, 128), BF16),
            pltpu.VMEM((QUADS, NZ, 16, 128), BF16),
            pltpu.VMEM((QUADS, NZ - 1, 16, 128), BF16),
            dma((3,)),
            dma((QUADS, 2)),
            dma((QUADS, 2, 2)),
            dma((QUADS, 2, 2)),
            dma((QUADS, 2)),
            dma((QUADS, 2)),
            dma((QUADS, NZ - 1)),
            dma((QUADS, NZ - 1)),
            dma((QUADS, NZ - 1)),
            dma((QUADS, NZ - 1)),
        ],
        compiler_params=pltpu.CompilerParams(
            collective_id=0, has_side_effects=True, vmem_limit_bytes=56 * 1024 * 1024
        ),
    )(queries, latent_kv, pair_blocks, pair_count, obs_count, cotangent)
    return pl.pallas_call(
        hand_out,
        out_shape=tuple(jax.ShapeDtypeStruct(r.shape, r.dtype) for r in results),
        in_specs=[hbm] * 3,
        out_specs=(hbm,) * 3,
        scratch_shapes=[pltpu.VMEM(r.shape, r.dtype) for r in results] + [dma((2, 3))],
        compiler_params=pltpu.CompilerParams(vmem_limit_bytes=60 * 1024 * 1024),
    )(*results)


def solution(mesh):
    placed = (
        P(("obs", "grid"), None),
        P("grid", None, None),
        P(("obs", "grid"), None),
        P(("obs", "grid")),
        P(("obs", "grid")),
        P(("obs", "grid"), None),
    )
    return jax.shard_map(
        per_device,
        mesh=mesh,
        in_specs=placed,
        out_specs=(P(("obs", "grid"), None), P(("obs", "grid"), None), P("grid", "obs", None)),
        check_vma=False,
    )
```

```python
import functools
import math

import jax
import jax.numpy as jnp
from jax import lax
from jax.experimental import pallas as pl
from jax.experimental.pallas import tpu as pltpu
from jax.sharding import PartitionSpec as P

H = 16
HEAD = 64
NY, NZ = 8, 12
BLOCK = 128
WIN = 5
QUADS = 4
HEADS = H // QUADS
QUAD = HEADS * HEAD
MESH = pl.DeviceIdType.MESH
SCALE = 1.0 / math.sqrt(HEAD)
LOG2E = 1.4426950408889634
F32, BF16 = jnp.float32, jnp.bfloat16
HALO_QUADS = ((0, 1), (1, 1), (2, 2))
FIRST_AXIS = ("z", "y", "z", "y")
TURN = (1, 1, -1, -1)
RUNS = (
    ((1, 6, 5), (1, 4, 3), (1, 2, 1), (-1, 5, 4), (-1, 3, 2), (-1, 1, 1)),
    ((1, 4, 3), (1, 2, 1), (-1, 3, 2), (-1, 1, 1)),
    ((1, 6, 5), (1, 4, 3), (1, 2, 1), (-1, 5, 4), (-1, 3, 2), (-1, 1, 1)),
    ((1, 4, 3), (1, 2, 1), (-1, 3, 2), (-1, 1, 1)),
)


def dot(a, b):
    return jnp.dot(a, b, preferred_element_type=F32)


def slot_bias(blocks_ref, count_ref, region, n, w, total):
    wanted = lax.rem(3 * region - 1 + w + total, total)
    uses = 0
    for p in range(blocks_ref.shape[1]):
        live = (blocks_ref[n, p] == wanted) & (p < count_ref[n])
        uses = uses + jnp.where(live, 1, 0)
    return jnp.where(
        uses == 0,
        F32(-1e30),
        jnp.where(
            uses == 1,
            F32(0.0),
            jnp.where(uses == 2, F32(1.0), jnp.where(uses == 3, F32(math.log2(3.0)), F32(2.0))),
        ),
    )


def owner_tiles(keys, values):
    rows = keys.shape[0]
    low = lax.broadcasted_iota(jnp.int32, (rows // 8, 8, 128), 1) < 4

    def split(a, lane):
        return a[:, lane : lane + 128].reshape(rows // 8, 8, 128)

    def pair(a):
        left, right = split(a, 0), split(a, 128)
        even = jnp.where(low, left, pltpu.roll(right, 4, 1))
        odd = jnp.where(low, pltpu.roll(left, 4, 1), right)
        return even, odd

    key_even, key_odd = pair(keys)
    value_even, value_odd = pair(values)
    even = jnp.concatenate([key_even, value_even], axis=1)
    odd = jnp.concatenate([key_odd, value_odd], axis=1)
    return jnp.stack([even, odd], axis=1).reshape(rows // 4, 16, 128)


def kernel(
    queries, latent, blocks, pair_count, obs_count, cotangent,
    attended, grad_query, grad_kv,
    query_in, grad_in, mixed_out, query_grad_out, lows, grad_lows, window, middle,
    rim_out, rim_in, part, first_in, hop_out, second_out, second_in,
    local_sem, store_sem, halo_send, halo_recv, rim_send, rim_recv,
    first_send, first_recv, second_send, second_recv,
):
    place, region = lax.axis_index("obs"), lax.axis_index("grid")
    regions = lax.axis_size("grid")
    y, z = place // NZ, lax.rem(place, NZ)
    after = (place, lax.rem(region + 1, regions))
    before = (place, lax.rem(region + regions - 1, regions))

    def around(at, k, size):
        moved = at + k % size
        return jnp.where(moved >= size, moved - size, moved)

    at_y = [around(y, k, NY) for k in range(NY)]
    at_z = [around(z, k, NZ) for k in range(NZ)]
    place_y = [i * NZ + z for i in at_y]
    place_z = [y * NZ + i for i in at_z]

    def along(axis, k):
        return at_y[k % NY] if axis == "y" else at_z[k % NZ]

    def peer(axis, k):
        return (place_y[k % NY] if axis == "y" else place_z[k % NZ], region)

    peers = [peer("y", k) for k in range(1, NY)] + [peer("z", k) for k in range(1, NZ)]
    barrier = pltpu.get_barrier_semaphore()
    for device in [after, before] + peers:
        pl.semaphore_signal(barrier, inc=1, device_id=device, device_id_type=MESH)

    loads = [
        pltpu.make_async_copy(latent.at[0], window.at[pl.ds(BLOCK, 3 * BLOCK)], local_sem.at[0]),
        pltpu.make_async_copy(queries, query_in, local_sem.at[1]),
        pltpu.make_async_copy(cotangent, grad_in, local_sem.at[2]),
    ]
    for copy in loads:
        copy.start()
    pl.semaphore_wait(barrier, 2 + len(peers))

    def halo_copies(g):
        copies = []
        first_quad, count = HALO_QUADS[g]
        for part_at in range(2):
            columns = pl.ds(part_at * H * HEAD + first_quad * QUAD, count * QUAD)
            for side, device in enumerate((after, before)):
                source = 2 * BLOCK if side == 0 else 0
                target = 0 if side == 0 else 4 * BLOCK
                copies.append(
                    pltpu.make_async_remote_copy(
                        src_ref=latent.at[0, pl.ds(source, BLOCK), columns],
                        dst_ref=window.at[pl.ds(target, BLOCK), columns],
                        send_sem=halo_send.at[g, part_at, side],
                        recv_sem=halo_recv.at[g, part_at, side],
                        device_id=device,
                        device_id_type=MESH,
                    )
                )
        return copies

    halos = [halo_copies(g) for g in range(len(HALO_QUADS))]
    for copies in halos:
        for copy in copies:
            copy.start()

    lane = lax.broadcasted_iota(jnp.int32, (1, 2 * BLOCK), 1)
    in_first = lane < BLOCK
    bias = [
        jnp.where(
            in_first,
            slot_bias(blocks, pair_count, region, 0, w, 3 * regions),
            slot_bias(blocks, pair_count, region, 1, w, 3 * regions),
        )
        for w in range(WIN)
    ]
    lane_live = lane < jnp.where(in_first, obs_count[0], BLOCK + obs_count[1])
    row = lax.broadcasted_iota(jnp.int32, (2 * BLOCK, 1), 0)
    row_live = row < jnp.where(row < BLOCK, obs_count[0], BLOCK + obs_count[1])
    head_lane = lax.broadcasted_iota(jnp.int32, (2 * BLOCK, QUAD), 1) // HEAD

    def compute(g):
        columns = pl.ds(g * QUAD, QUAD)
        value_columns = pl.ds(H * HEAD + g * QUAD, QUAD)
        query = query_in[:, columns]
        grad = jnp.where(row_live, grad_in[:, columns], 0).astype(BF16)
        query_t, grad_t = query.T, grad.T
        keys, values = window[:, columns], window[:, value_columns]
        def alone(a, h):
            rows = slice(h * HEAD, (h + 1) * HEAD)
            pieces = []
            if h > 0:
                pieces.append(jnp.zeros((h * HEAD, a.shape[1]), a.dtype))
            pieces.append(a[rows])
            if h < HEADS - 1:
                pieces.append(jnp.zeros(((HEADS - 1 - h) * HEAD, a.shape[1]), a.dtype))
            return jnp.concatenate(pieces, axis=0)

        def front(h):
            return dot(keys, alone(query_t, h)), dot(values, alone(grad_t, h))

        ready = front(0)
        for h in range(HEADS):
            scores, grad_attention = ready
            if h < HEADS - 1:
                ready = front(h + 1)
            tops = [
                jnp.max(scores[w * BLOCK : (w + 1) * BLOCK], axis=0, keepdims=True) * (SCALE * LOG2E) + bias[w]
                for w in range(WIN)
            ]
            top = functools.reduce(jnp.maximum, tops)
            shift = jnp.concatenate(
                [jnp.broadcast_to(top - bias[w], (BLOCK, 2 * BLOCK)) for w in range(WIN)], axis=0
            )
            expanded = jnp.exp2(scores * (SCALE * LOG2E) - shift)
            attention = expanded * (1.0 / jnp.sum(expanded, axis=0, keepdims=True))
            attention_low = attention.astype(BF16)
            delta = jnp.sum(attention * grad_attention, axis=0, keepdims=True)
            grad_low = (attention * ((grad_attention - delta) * SCALE)).astype(BF16)
            lows[g * HEADS + h] = attention_low
            grad_lows[g * HEADS + h] = grad_low

        def spread(a):
            return jnp.concatenate([jnp.where(head_lane == h, a, 0).astype(BF16) for h in range(HEADS)], axis=0)

        query_spread, grad_spread = spread(query), spread(grad)

        def grad_tiles(start, count):
            at = slice(start * BLOCK, (start + count) * BLOCK)

            def heads(ref):
                return jnp.concatenate([ref[g * HEADS + h, at] for h in range(HEADS)], axis=1)

            return owner_tiles(dot(heads(grad_lows), query_spread), dot(heads(lows), grad_spread))

        rim_out[g, 0] = grad_tiles(0, 1).astype(BF16)
        rim_out[g, 1] = grad_tiles(4, 1).astype(BF16)
        rims[g] = rim_copies(g)
        for copy in rims[g]:
            copy.start()
        middle[g] = grad_tiles(1, 3)

    def hand_over(g):
        columns = pl.ds(g * QUAD, QUAD)
        keys_t = window[:, columns].T
        values_t = window[:, pl.ds(H * HEAD + g * QUAD, QUAD)].T
        mixed, query_grads = [], []
        for h in range(HEADS):
            rows = slice(h * HEAD, (h + 1) * HEAD)
            mixed.append(dot(values_t[rows], lows[g * HEADS + h]))
            query_grads.append(dot(keys_t[rows], grad_lows[g * HEADS + h]))
        mixed = jnp.where(lane_live, jnp.concatenate(mixed, axis=0), 0.0)
        mixed_out[:, columns] = mixed.T.astype(BF16)
        query_grad_out[:, columns] = jnp.concatenate(query_grads, axis=0).T.astype(BF16)
        for i, (held, result) in enumerate(((mixed_out, attended), (query_grad_out, grad_query))):
            copy = pltpu.make_async_copy(held.at[:, columns], result.at[:, columns], store_sem.at[g, i])
            copy.start()
            stores.append(copy)

    def rim_copies(g):
        return [
            pltpu.make_async_remote_copy(
                src_ref=rim_out.at[g, side],
                dst_ref=rim_in.at[g, side],
                send_sem=rim_send.at[g, side],
                recv_sem=rim_recv.at[g, side],
                device_id=device,
                device_id_type=MESH,
            )
            for side, device in enumerate((before, after))
        ]

    def exchange(axis, source, target, send, recv):
        copies = []
        size = NY if axis == "y" else NZ
        for k in sorted(range(1, size), key=lambda k: -min(k, size - k)):
            copies.append(
                pltpu.make_async_remote_copy(
                    src_ref=source(along(axis, k)),
                    dst_ref=target(k - 1),
                    send_sem=send(k - 1),
                    recv_sem=recv(k - 1),
                    device_id=peer(axis, k),
                    device_id_type=MESH,
                )
            )
        return copies

    def piece(g, axis, i):
        return part.at[g, i] if axis == "y" else part.at[g, :, i]

    def landing(g, axis, k):
        if axis == "y":
            return first_in.at[g, k, pl.ds(0, NZ)]
        return first_in.at[g, k, pl.ds(0, NY)]

    def first_copy(g, axis, source, k, slot):
        return pltpu.make_async_remote_copy(
            src_ref=source,
            dst_ref=landing(g, axis, slot),
            send_sem=first_send.at[g, slot],
            recv_sem=first_recv.at[g, slot],
            device_id=peer(axis, k),
            device_id_type=MESH,
        )

    def runs_of(g):
        axis, turn = FIRST_AXIS[g], TURN[g]
        runs, at = [], 0
        hops = sum(far - near for _, far, near in RUNS[g])
        for n, (sign, far, near) in enumerate(RUNS[g]):
            runs.append((turn * sign, tuple(range(far, near - 1, -1)), at, hops + n))
            at += far - near
        return axis, runs, hops

    def send_step(g, step, source_of):
        axis, runs, _ = runs_of(g)
        for run, (sign, distances, at, last) in enumerate(runs):
            if step >= len(distances):
                continue
            source = source_of(axis, run, sign * distances[step], at + step - 1)
            if step == len(distances) - 1:
                copy = first_copy(g, axis, source, sign * distances[step], last)
            else:
                copy = first_copy(g, axis, source, sign, at + step)
            copy.start()
            firsts[g][last if step == len(distances) - 1 else at + step] = copy

    def second_copies(g):
        axis = "z" if FIRST_AXIS[g] == "y" else "y"
        return exchange(
            axis,
            lambda i: second_out.at[g, i],
            lambda k: second_in.at[g, k],
            lambda k: second_send.at[g, k],
            lambda k: second_recv.at[g, k],
        )

    def start_first(g, rims):
        for copy in rims:
            copy.wait_recv()
        half = part.at[g]
        for i in range(NY):
            owned = middle[g, i * NZ : (i + 1) * NZ]
            for side, start in ((1, 0), (0, 64)):
                low, high = max(i * NZ, start), min((i + 1) * NZ, start + 32)
                if low < high:
                    extra = rim_in[g, side, low - start : high - start].astype(F32)
                    pieces = [extra]
                    if low > i * NZ:
                        pieces.insert(0, jnp.zeros((low - i * NZ, 16, 128), F32))
                    if high < (i + 1) * NZ:
                        pieces.append(jnp.zeros(((i + 1) * NZ - high, 16, 128), F32))
                    owned = owned + jnp.concatenate(pieces, axis=0)
            half[i] = owned.astype(BF16)
        firsts[g] = {}
        send_step(g, 0, lambda axis, run, at, slot: piece(g, axis, along(axis, at)))

    def pass_on(g, step):
        def source_of(axis, run, at, slot):
            firsts[g][slot].wait_recv()
            total = piece(g, axis, along(axis, at))[...].astype(F32) + landing(g, axis, slot)[...].astype(F32)
            staged = hop_out.at[g, slot, pl.ds(0, total.shape[0])]
            staged[...] = total.astype(BF16)
            return staged

        send_step(g, step, source_of)

    def start_second(g):
        axis, runs, hops = runs_of(g)
        mine = along(axis, 0)
        total = piece(g, axis, mine)[...].astype(F32)
        for k in range(hops, hops + len(runs)):
            firsts[g][k].wait_recv()
            total = total + landing(g, axis, k)[...].astype(F32)
        count = total.shape[0]
        second_out[g, 0:count] = total.astype(BF16)
        copies = second_copies(g)
        for copy in copies:
            copy.start()
        return copies

    def finish(g, copies):
        for copy in copies:
            copy.wait_recv()
        axis = "z" if FIRST_AXIS[g] == "y" else "y"
        total = second_out[g, along(axis, 0)].astype(F32)
        for k in range(len(copies)):
            total = total + second_in[g, k].astype(F32)
        for c in range(4):
            start = (c // 2) * H * HEAD + g * QUAD + (c % 2) * 128
            grad_kv[0, :, start : start + 128] = total[4 * c : 4 * c + 4]

    for copy in loads:
        copy.wait()
    rims, firsts, seconds, stores = {}, {}, {}, []

    def front(g):
        if g < len(HALO_QUADS):
            for copy in halos[g]:
                copy.wait_recv()
        compute(g)

    def first(g):
        start_first(g, rims[g])

    def second(g):
        seconds[g] = start_second(g)

    plan = (
        (front, 0), (front, 1), (front, 2), (first, 0), (front, 3), (first, 1), (hand_over, 0), (first, 2), (pass_on, 0, 1), (hand_over, 1),
        (first, 3), (pass_on, 1, 1), (hand_over, 2), (pass_on, 2, 1), (hand_over, 3), (pass_on, 3, 1),
        (second, 0), (second, 1), (second, 3), (second, 2),
    )
    for step, *at in plan:
        step(*at)
    for g in range(QUADS):
        finish(g, seconds[g])
    for copy in stores:
        copy.wait()
    hops = [list(copies.values()) for copies in firsts.values()]
    for groups in (halos, rims.values(), hops, seconds.values()):
        for copies in groups:
            for copy in copies:
                copy.wait_send()


def hand_out(*refs):
    sources, targets, held, sems = refs[:3], refs[3:6], refs[6:9], refs[9]
    loads = [pltpu.make_async_copy(a, b, sems.at[0, i]) for i, (a, b) in enumerate(zip(sources, held))]
    stores = [pltpu.make_async_copy(a, b, sems.at[1, i]) for i, (a, b) in enumerate(zip(held, targets))]
    for copy in loads:
        copy.start()
    for load, store in zip(loads, stores):
        load.wait()
        store.start()
    for copy in stores:
        copy.wait()


def per_device(queries, latent_kv, pair_blocks, pair_count, obs_count, cotangent):
    vmem = pl.BlockSpec(memory_space=pltpu.VMEM)
    smem = pl.BlockSpec(memory_space=pltpu.SMEM)
    hbm = pl.BlockSpec(memory_space=pl.ANY)
    rows, width = queries.shape
    dma = pltpu.SemaphoreType.DMA
    results = pl.pallas_call(
        kernel,
        out_shape=(
            jax.ShapeDtypeStruct((rows, width), BF16),
            jax.ShapeDtypeStruct((rows, width), BF16),
            jax.ShapeDtypeStruct((1, 4, 2 * width), F32),
        ),
        in_specs=[hbm, hbm, smem, smem, smem, hbm],
        out_specs=(hbm, hbm, vmem),
        scratch_shapes=[
            pltpu.VMEM((rows, width), BF16),
            pltpu.VMEM((rows, width), BF16),
            pltpu.VMEM((rows, width), BF16),
            pltpu.VMEM((rows, width), BF16),
            pltpu.VMEM((H, WIN * BLOCK, rows), BF16),
            pltpu.VMEM((H, WIN * BLOCK, rows), BF16),
            pltpu.VMEM((WIN * BLOCK, 2 * width), BF16),
            pltpu.VMEM((QUADS, NY * NZ, 16, 128), F32),
            pltpu.VMEM((QUADS, 2, 32, 16, 128), BF16),
            pltpu.VMEM((QUADS, 2, 32, 16, 128), BF16),
            pltpu.VMEM((QUADS, NY, NZ, 16, 128), BF16),
            pltpu.VMEM((QUADS, NZ - 1, NZ, 16, 128), BF16),
            pltpu.VMEM((QUADS, NZ, NZ, 16, 128), BF16),
            pltpu.VMEM((QUADS, NZ, 16, 128), BF16),
            pltpu.VMEM((QUADS, NZ - 1, 16, 128), BF16),
            dma((3,)),
            dma((QUADS, 2)),
            dma((QUADS, 2, 2)),
            dma((QUADS, 2, 2)),
            dma((QUADS, 2)),
            dma((QUADS, 2)),
            dma((QUADS, NZ - 1)),
            dma((QUADS, NZ - 1)),
            dma((QUADS, NZ - 1)),
            dma((QUADS, NZ - 1)),
        ],
        compiler_params=pltpu.CompilerParams(
            collective_id=0, has_side_effects=True, vmem_limit_bytes=56 * 1024 * 1024
        ),
    )(queries, latent_kv, pair_blocks, pair_count, obs_count, cotangent)
    return pl.pallas_call(
        hand_out,
        out_shape=tuple(jax.ShapeDtypeStruct(r.shape, r.dtype) for r in results),
        in_specs=[hbm] * 3,
        out_specs=(hbm,) * 3,
        scratch_shapes=[pltpu.VMEM(r.shape, r.dtype) for r in results] + [dma((2, 3))],
        compiler_params=pltpu.CompilerParams(vmem_limit_bytes=60 * 1024 * 1024),
    )(*results)


def solution(mesh):
    placed = (
        P(("obs", "grid"), None),
        P("grid", None, None),
        P(("obs", "grid"), None),
        P(("obs", "grid")),
        P(("obs", "grid")),
        P(("obs", "grid"), None),
    )
    return jax.shard_map(
        per_device,
        mesh=mesh,
        in_specs=placed,
        out_specs=(P(("obs", "grid"), None), P(("obs", "grid"), None), P("grid", "obs", None)),
        check_vma=False,
    )
```
